256 devices in a mesh: seq: 64 (over x, y, z_hi), ch: 4 (over z_lo, core).
Axes of the slice: x: 4, y: 4, z: 8 (z_hi: 4, z_lo: 2; z = z_hi * 2 + z_lo), core: 2. Of those that a mesh axis runs over, the one named last changes fastest.
Arguments:
- value_rows: float32 [8192, 4096], P('seq', 'ch'), may hold values from -6 to 6
- key_rows: float32 [8192, 4096], P('seq', 'ch'), may hold values from -6 to 6
- query_rows: float32 [8192, 4096], P('seq', 'ch'), may hold values from -6 to 6
- pole_weights: float32 [16, 4096], P(None, 'ch'), may hold values from -0.225 to 0.225, as said below
- damping_speeds: float32 [16, 4096], P(None, 'ch'), may hold values from 6.1035156e-05 to 0.1, as said below
- out_weight: bfloat16 [4096, 4096], P('ch'), may hold values from -0.125 to 0.125
Outputs:
- mixed: bfloat16 [8192, 4096], P('seq', 'ch')
The draws below stay inside these ranges and needn't reach their ends.
Inputs may be any that keep to these rules, and one draw needn't show every extreme that they name: `pole_weights`: amplitudes of the modes. `damping_speeds`: decay rates per position.
All inputs are finite; a program needn't handle non-finite values.
Results may differ from the reference program's by a relative error of at most 0.005.
Values sent between devices are 32-bit elements; how exact they have to be, the bound alone decides.
No kernel may reach another device: no remote copies, remote signals or barrier semaphores. Data moves between devices by JAX's collectives and lax.ppermute only.
A program may use at most 64 MiB of HBM per device.

```python
import math
import jax
import jax.numpy as jnp
from jax import lax

C = 4096
DO = 4096
MODES = 16
TOKENS = 8192


def draw_pole_weights(key, part):
    key = jax.random.fold_in(key, 29)
    sign_key, size_key = jax.random.split(key)
    signs = (2 * jax.random.randint(sign_key, (1, C), 0, 2) - 1).astype(jnp.float32)
    spread = jax.random.uniform(size_key, (MODES, C), jnp.float32)
    magnitude = 0.5 + spread
    return (0.15 * signs * magnitude).astype(jnp.float32)


def draw_damping_speeds(key, part):
    key = jax.random.fold_in(key, 17)
    band_key, place_key = jax.random.split(key)
    band_index = jax.random.randint(band_key, (MODES, C), 0, 8)
    position = jax.random.uniform(place_key, (MODES, C), jnp.float32)
    slow_lower = 0.5 / TOKENS
    slow_upper = 2.0 / TOKENS
    lower_ends = jnp.where(band_index < 2, slow_lower, jnp.where(band_index < 6, 0.003, jnp.where(band_index < 7, 0.015, 0.05)))
    upper_ends = jnp.where(band_index < 2, slow_upper, jnp.where(band_index < 6, 0.015, jnp.where(band_index < 7, 0.05, 0.1)))
    lower_ends = lower_ends.astype(jnp.float32)
    upper_ends = upper_ends.astype(jnp.float32)
    return (lower_ends * jnp.exp(position * jnp.log(upper_ends / lower_ends))).astype(jnp.float32)


def strengthened(result, rng, source, target, parts, factor):
    owner, partner = [(jnp.arange(result.shape[dim]) // (result.shape[dim] // parts)).reshape([-1 if axis == dim else 1 for axis in range(result.ndim)]) for dim in (source, target)]
    chosen = jax.random.permutation(rng, parts)[partner]
    strong = (owner == chosen) | (owner == (partner + parts // 2) % parts)
    return jnp.where(strong, factor * result, result)


def shard_levels(own_key, extent, cuts, smallest, top_value):
    gain, own = 1.0, jax.random.fold_in(own_key, 6)
    for axis_at, parts in cuts:
        heights = jnp.exp(jax.random.uniform(jax.random.fold_in(own, axis_at), (parts,), jnp.float32, smallest / len(cuts), top_value / len(cuts)))
        gain = gain * jnp.repeat(heights, extent[axis_at] // parts).reshape([-1 if axis == axis_at else 1 for axis in range(len(extent))])
    return gain


def normal_values(own_key, extent, deviation, reach, cuts=(), held_as=jnp.bfloat16):
    factor_of = shard_levels(own_key, extent, cuts, -0.22, 0.18) if cuts else 1.0
    entries = jax.random.normal(own_key, extent, jnp.float32) * deviation * factor_of
    return jnp.minimum(jnp.maximum(entries, -reach), reach).astype(held_as)


def gaussian_with(own_key, shape, deviation, reach, cuts, heavy, kind=jnp.bfloat16):
    result = deviation * jax.random.normal(own_key, shape, jnp.float32)
    if cuts:
        result = result * shard_levels(own_key, shape, cuts, -0.22, 0.18)
    return jnp.clip(strengthened(result, jax.random.fold_in(own_key, 3), *heavy), -reach, reach).astype(kind)


def setup_inputs(seed: int = 0) -> dict:
    streams_of = jax.random.split(jax.random.key(seed), 7)
    value_rows = normal_values(streams_of[0], (TOKENS, C), 1.0, 6.0, ((0, 64), (1, 4)), jnp.float32)
    key_rows = normal_values(streams_of[1], (TOKENS, C), 1.0, 6.0, ((0, 64), (1, 4)), jnp.float32)
    query_rows = normal_values(streams_of[2], (TOKENS, C), 1.0, 6.0, ((0, 64), (1, 4)), jnp.float32)
    pole_weights = draw_pole_weights(jax.random.fold_in(streams_of[6], 71), 0)
    damping_speeds = draw_damping_speeds(jax.random.fold_in(streams_of[6], 71), 0)
    out_weight = gaussian_with(streams_of[5], (C, DO), C ** -0.5, 0.125, ((0, 4),), (0, 1, 4, 2.0))
    return dict(value_rows=value_rows, key_rows=key_rows, query_rows=query_rows, pole_weights=pole_weights, damping_speeds=damping_speeds, out_weight=out_weight)


def pole_kernel(pole_damping, pole_gains, step_moments):
    projector_coefficients = pole_gains * jnp.sqrt(-jnp.expm1(-2.0 * pole_damping))

    def add_pole_term(partial_sum, piece_collection):
        return (partial_sum + piece_collection[1][None, :] * jnp.exp(-piece_collection[0][None, :] * step_moments[:, None]), None)
    layer_result, ignored_entry = lax.scan(add_pole_term, jnp.zeros((step_moments.shape[0], pole_damping.shape[1]), jnp.float32), (pole_damping, projector_coefficients))
    return layer_result

def reference(value_rows, key_rows, query_rows, pole_weights, damping_speeds, out_weight):
    context_span = value_rows.shape[0]
    step_moments = jnp.arange(context_span, dtype=jnp.float32)
    kernel_family = pole_kernel(damping_speeds, pole_weights, step_moments)
    signal = key_rows * value_rows
    channel_count = signal.shape[1]
    block_width = math.gcd(channel_count, 256)
    block_count = channel_count // block_width

    def convolve(piece_collection):
        spectrum = jnp.fft.rfft(piece_collection[0], n=2 * context_span, axis=0) * jnp.fft.rfft(piece_collection[1], n=2 * context_span, axis=0)
        return jnp.fft.irfft(spectrum, n=2 * context_span, axis=0)[:context_span]
    stacked = (signal.reshape(context_span, block_count, block_width).transpose(1, 0, 2), kernel_family.reshape(context_span, block_count, block_width).transpose(1, 0, 2))
    convolved = lax.map(convolve, stacked).transpose(1, 0, 2).reshape(context_span, channel_count)
    gated = (query_rows * convolved).astype(jnp.bfloat16)
    return jnp.dot(gated, out_weight, preferred_element_type=jnp.float32).astype(jnp.bfloat16)
```

```python
import jax
import jax.numpy as jnp
from jax import lax
from jax.experimental import pallas as pl
from jax.experimental.pallas import tpu as pltpu
from jax.sharding import PartitionSpec as P

MODES = 16
GROUPS = 8
LANES = 128


def tiles(array):
    rows, columns = array.shape
    cut = array.reshape(rows // 8, 8, columns // LANES, LANES)
    return cut.transpose(0, 2, 1, 3).reshape(rows // 8, 8 * (columns // LANES), LANES)


def row(ref, outer, inner):
    return ref[outer, pl.ds(inner, GROUPS, stride=8), :]


def mode(index):
    return pl.ds(index * GROUPS, GROUPS)


def end_state_kernel(key_ref, value_ref, damping_ref, signal_ref, state_ref, flat_ref):
    decay = []
    for m in range(MODES):
        damping = row(damping_ref, m // 8, m % 8)
        flat_ref[mode(m), :] = damping
        decay.append(jnp.exp(-damping))

    def body(outer, state):
        for inner in range(8):
            signal = row(key_ref, outer, inner) * row(value_ref, outer, inner)
            signal_ref[outer, pl.ds(inner * GROUPS, GROUPS), :] = signal
            state = tuple(decay[m] * state[m] + signal for m in range(MODES))
        return state

    zero = jnp.zeros((GROUPS, LANES), jnp.float32)
    state = lax.fori_loop(0, key_ref.shape[0], body, (zero,) * MODES)
    for m in range(MODES):
        state_ref[mode(m), :] = state[m]


def local_kernel(signal_ref, flat_ref, gain_ref, out_ref):
    decay = [jnp.exp(-flat_ref[mode(m), :]) for m in range(MODES)]
    gain = [row(gain_ref, m // 8, m % 8) for m in range(MODES)]

    def body(outer, state):
        for inner in range(8):
            signal = signal_ref[outer, pl.ds(inner * GROUPS, GROUPS), :]
            state = tuple(decay[m] * state[m] + signal for m in range(MODES))
            terms = [gain[m] * state[m] for m in range(MODES)]
            while len(terms) > 1:
                terms = [terms[n] + terms[n + 1] for n in range(0, len(terms), 2)]
            out_ref[outer, pl.ds(inner * GROUPS, GROUPS), :] = terms[0]
        return state

    zero = jnp.zeros((GROUPS, LANES), jnp.float32)
    lax.fori_loop(0, signal_ref.shape[0], body, (zero,) * MODES)


def gate_kernel(query_ref, local_ref, flat_ref, gain_ref, entry_ref, out_ref, rows_ref):
    decay = [jnp.exp(-flat_ref[mode(m), :]) for m in range(MODES)]
    state = tuple(
        row(gain_ref, m // 8, m % 8) * entry_ref[mode(m), :] for m in range(MODES)
    )

    def body(outer, state):
        for inner in range(8):
            state = tuple(decay[m] * state[m] for m in range(MODES))
            terms = list(state) + [local_ref[outer, pl.ds(inner * GROUPS, GROUPS), :]]
            while len(terms) > 1:
                terms = [
                    terms[n] + terms[n + 1] if n + 1 < len(terms) else terms[n]
                    for n in range(0, len(terms), 2)
                ]
            rows_ref[outer, pl.ds(inner, GROUPS, stride=8), :] = (
                row(query_ref, outer, inner) * terms[0]
            )
        return state

    lax.fori_loop(0, query_ref.shape[0], body, state)
    for g in range(GROUPS):
        block = rows_ref[:, pl.ds(8 * g, 8), :].reshape(out_ref.shape[0], LANES)
        out_ref[:, pl.ds(g * LANES, LANES)] = block.astype(jnp.bfloat16)


def vmem(count):
    return [pl.BlockSpec(memory_space=pltpu.VMEM)] * count


def f32(*shape):
    return jax.ShapeDtypeStruct(shape, jnp.float32)


def cost(flops, size):
    return pl.CostEstimate(flops=flops, bytes_accessed=size, transcendentals=0)


def partner_pairs(size, step):
    return [(i, i ^ step) for i in range(size)]


def prefix(state, damping, place, unit, wants_total):
    here = lax.rem(lax.div(lax.axis_index("seq"), place), 4)
    count = lax.axis_size("seq")

    def decayed(values, steps):
        return values * jnp.exp(damping * (-unit * steps.astype(jnp.float32)))

    entering = jnp.zeros_like(state)
    total = decayed(state, 3 - here)
    for step in (2, 1, 3):
        there = here ^ step
        other = lax.ppermute(state, "seq", partner_pairs(count, step * place))
        ahead = jnp.maximum(here - there - 1, 0)
        entering = entering + jnp.where(there < here, decayed(other, ahead), 0.0)
        total = total + decayed(other, 3 - there)
    return entering, (total if wants_total else None), here


def local(value_rows, key_rows, query_rows, pole_weights, damping_speeds, out_weight):
    rows, channels = value_rows.shape
    outer = rows // 8
    signal, state, damping = pl.pallas_call(
        end_state_kernel,
        out_shape=(
            f32(outer, 64, LANES),
            f32(MODES * GROUPS, LANES),
            f32(MODES * GROUPS, LANES),
        ),
        in_specs=vmem(3),
        out_specs=tuple(vmem(3)),
        cost_estimate=cost(5_000_000, 2_000_000),
    )(tiles(key_rows), tiles(value_rows), tiles(damping_speeds))
    gain = tiles(pole_weights * jnp.sqrt(-jnp.expm1(-2.0 * damping_speeds)))
    near = pl.pallas_call(
        local_kernel,
        out_shape=f32(outer, 64, LANES),
        in_specs=vmem(3),
        out_specs=vmem(1)[0],
        cost_estimate=cost(10_000_000, 1_000_000),
    )(signal, damping, gain)

    from_z, total, z = prefix(state, damping, 1, float(rows), True)
    from_y, total, y = prefix(total, damping, 4, 4.0 * rows, True)
    from_x, _, x = prefix(total, damping, 16, 16.0 * rows, False)
    far = from_y + from_x * jnp.exp(damping * (-4.0 * rows * y.astype(jnp.float32)))
    entry = from_z + far * jnp.exp(damping * (-1.0 * rows * z.astype(jnp.float32)))

    gated = pl.pallas_call(
        gate_kernel,
        out_shape=jax.ShapeDtypeStruct((rows, channels), jnp.bfloat16),
        in_specs=vmem(5),
        out_specs=vmem(1)[0],
        scratch_shapes=[pltpu.VMEM((outer, 64, LANES), jnp.float32)],
        cost_estimate=cost(6_000_000, 2_000_000),
    )(tiles(query_rows), near, damping, gain, entry)

    own = lax.axis_index("ch")
    width = out_weight.shape[1] // lax.axis_size("ch")
    core_swap = partner_pairs(4, 1)
    chip_swap = partner_pairs(4, 2)

    def weight_of(group):
        return lax.dynamic_slice_in_dim(out_weight, group * width, width, axis=1)

    def project(weight):
        return jnp.dot(gated, weight, preferred_element_type=jnp.float32)

    def chip_sum(kept, sent, parts):
        kept, sent = weight_of(kept), weight_of(sent)
        sums = []
        for n in range(parts):
            cut = slice(n * width // parts, (n + 1) * width // parts)
            arrived = lax.ppermute(project(sent[:, cut]), "ch", core_swap)
            sums.append(project(kept[:, cut]) + arrived)
        return sums

    parts = 2
    away = chip_sum(own ^ 2, own ^ 3, parts)
    away = [lax.ppermute(piece, "ch", chip_swap) for piece in away]
    home = chip_sum(own, own ^ 1, parts)
    return jnp.concatenate(
        [(a + b).astype(jnp.bfloat16) for a, b in zip(home, away)], axis=1
    )


def solution(mesh):
    in_specs = (
        P("seq", "ch"),
        P("seq", "ch"),
        P("seq", "ch"),
        P(None, "ch"),
        P(None, "ch"),
        P("ch", None),
    )
    return jax.shard_map(
        local, mesh=mesh, in_specs=in_specs, out_specs=P("seq", "ch"), check_vma=False
    )
```

```python
import jax
import jax.numpy as jnp
from jax import lax
from jax.experimental import pallas as pl
from jax.experimental.pallas import tpu as pltpu
from jax.sharding import PartitionSpec as P

MODES = 16
HALVES = MODES // 8
LANES = 128
SCOPE = 12 * 1024 * 1024
STEPS = (1, 3, 2)


def tiles(array):
    rows, columns = array.shape
    cut = array.reshape(rows // 8, 8, columns // LANES, LANES)
    return cut.transpose(0, 2, 1, 3).reshape(rows // 8, 8 * (columns // LANES), LANES)


def spread(values, index):
    return jnp.broadcast_to(values[index : index + 1, :], (8, LANES))


def f32(*shape):
    return jax.ShapeDtypeStruct(shape, jnp.float32)


def kernel_call(body, out_shape, inputs, flops, size, scratch=()):
    outs = jax.tree.map(lambda _: pl.BlockSpec(memory_space=pltpu.VMEM), out_shape)
    return pl.pallas_call(
        body,
        out_shape=out_shape,
        in_specs=[pl.BlockSpec(memory_space=pltpu.VMEM)] * len(inputs),
        out_specs=outs,
        scratch_shapes=scratch,
        cost_estimate=pl.CostEstimate(flops=flops, bytes_accessed=size, transcendentals=0),
        compiler_params=pltpu.CompilerParams(vmem_limit_bytes=SCOPE),
    )(*inputs)


def end_state_kernel(signal_ref, damping_ref, state_ref):
    outer, lanes = signal_ref.shape[0], signal_ref.shape[1] // 8
    place = lax.broadcasted_iota(jnp.int32, (8, LANES), 0)
    for g in range(lanes):
        block = pl.ds(8 * g, 8)
        signal = [signal_ref[i, block, :] for i in range(outer)]
        for half in range(HALVES):
            decay = jnp.exp(-damping_ref[half, block, :])
            result = None
            for m in range(8):
                once = spread(decay, m)
                twice = once * once
                four = twice * twice
                eight = four * four
                total = signal[0]
                for i in range(1, outer):
                    total = eight * total + signal[i]
                total = total + once * pltpu.roll(total, 1, 0)
                total = total + twice * pltpu.roll(total, 2, 0)
                total = total + four * pltpu.roll(total, 4, 0)
                if m != 7:
                    total = pltpu.roll(total, m + 1, 0)
                result = total if result is None else jnp.where(place == m, total, result)
            state_ref[half, block, :] = result


def local_kernel(signal_ref, damping_ref, gain_ref, out_ref):
    def row(ref, outer, inner):
        return ref[outer, pl.ds(inner, 8, stride=8), :]

    decay = [jnp.exp(-row(damping_ref, m // 8, m % 8)) for m in range(MODES)]
    gain = [row(gain_ref, m // 8, m % 8) for m in range(MODES)]

    def body(outer, state):
        for inner in range(8):
            signal = row(signal_ref, outer, inner)
            state = tuple(decay[m] * state[m] + signal for m in range(MODES))
            terms = [gain[m] * state[m] for m in range(MODES)]
            while len(terms) > 1:
                terms = [terms[n] + terms[n + 1] for n in range(0, len(terms), 2)]
            out_ref[outer, pl.ds(inner, 8, stride=8), :] = terms[0]
        return state

    zero = jnp.zeros((8, LANES), jnp.float32)
    lax.fori_loop(0, signal_ref.shape[0], body, (zero,) * MODES)


def places():
    at = lax.axis_index("seq")
    return [lax.rem(at, 4), lax.rem(lax.div(at, 4), 4), lax.div(at, 16)]


def run_kernel(axis, rows, damping_ref, out_ref):
    here = places()[axis]
    damping = damping_ref[...] * (-1.0 * rows * 4**axis)
    for n, step in enumerate((0, *STEPS)):
        there = here ^ step
        out_ref[n] = jnp.exp(damping * (3 - there).astype(jnp.float32))
        if step:
            ahead = jnp.maximum(here - there - 1, 0).astype(jnp.float32)
            before = (there < here).astype(jnp.float32)
            out_ref[3 + n] = jnp.exp(damping * ahead) * before


def last_kernel(rows, damping_ref, gain_ref, out_ref, near_ref, eight_ref, powers_ref):
    z, y, x = places()
    damping, gain = damping_ref[...], gain_ref[...]
    to_y = (z * rows).astype(jnp.float32)
    to_x = ((4 * y + z) * rows).astype(jnp.float32)
    near_ref[0] = gain
    near_ref[1] = gain * jnp.exp(-damping * to_y)
    for n, step in enumerate(STEPS):
        there = x ^ step
        ahead = jnp.maximum(x - there - 1, 0).astype(jnp.float32) * (16.0 * rows) + to_x
        before = (there < x).astype(jnp.float32)
        out_ref[n] = gain * jnp.exp(-damping * ahead) * before
    eight_ref[...] = jnp.exp(-8.0 * damping)
    since = 1.0 + lax.broadcasted_iota(jnp.int32, (8, LANES), 0).astype(jnp.float32)
    for g in range(damping.shape[1] // 8):
        for half in range(HALVES):
            part = damping_ref[half, 8 * g : 8 * g + 8, :]
            for m in range(8):
                powers_ref[8 * half + m, 8 * g : 8 * g + 8, :] = jnp.exp(
                    -spread(part, m) * since
                )


def project(gated_ref, weight_ref, pieces):
    own = lax.axis_index("ch")
    width = weight_ref.shape[1] // 4
    for out_ref, group, start in pieces:
        first = pl.multiple_of((own ^ group) * width + start, LANES)
        out_ref[...] = jnp.dot(
            gated_ref[...],
            weight_ref[:, pl.ds(first, out_ref.shape[1])],
            preferred_element_type=jnp.float32,
        )


def gate_kernel(pieces, *refs):
    query_ref, local_ref, powers_ref, eight_ref, base_ref, last_ref = refs[:6]
    arrived, weight_ref, gated_ref = refs[6:9], refs[9], refs[10]
    outs, state_ref = refs[11:-1], refs[-1]
    total = base_ref[...]
    for n in range(3):
        total = total + last_ref[n] * arrived[n][...]
    state_ref[...] = total
    outer, lanes = query_ref.shape[0], query_ref.shape[1] // 8

    def body(g, carry):
        block = pl.ds(pl.multiple_of(8 * g, 8), 8)
        rows = [local_ref[i, block, :] for i in range(outer)]
        for half in range(HALVES):
            entry, eight = state_ref[half, block, :], eight_ref[half, block, :]
            for m in range(8):
                term = spread(entry, m) * powers_ref[8 * half + m, block, :]
                factor = spread(eight, m)
                for i in range(outer):
                    rows[i] = rows[i] + term
                    if i + 1 < outer:
                        term = term * factor
        rows = [query_ref[i, block, :] * rows[i] for i in range(outer)]
        columns = pl.ds(pl.multiple_of(LANES * g, LANES), LANES)
        gated_ref[:, columns] = jnp.concatenate(rows, axis=0).astype(jnp.bfloat16)
        return carry

    lax.fori_loop(0, lanes, body, 0)
    project(gated_ref, weight_ref, [(o, *p) for o, p in zip(outs, pieces)])


def project_kernel(pieces, gated_ref, weight_ref, *outs):
    project(gated_ref, weight_ref, [(o, *p) for o, p in zip(outs, pieces)])


def run_own(axis, rows, damping_ref, state_ref, out_ref, own_ref):
    run_kernel(axis, rows, damping_ref, out_ref)
    own_ref[...] = out_ref[0] * state_ref[...]


def finish_kernel(*refs):
    *pieces, out_ref = refs
    half = len(pieces) // 2
    width = pieces[0].shape[1]
    for n in range(half):
        total = pieces[n][...] + pieces[half + n][...]
        out_ref[:, n * width : (n + 1) * width] = total.astype(jnp.bfloat16)


def partner_pairs(size, step):
    return [(i, i ^ step) for i in range(size)]


def local(value_rows, key_rows, query_rows, pole_weights, damping_speeds, out_weight):
    rows, channels = value_rows.shape
    count = lax.axis_size("seq")
    queries = tiles(query_rows)
    damping = tiles(damping_speeds)
    gain = tiles(pole_weights * jnp.sqrt(-jnp.expm1(-2.0 * damping_speeds)))
    shape = damping.shape

    def swap(state, axis):
        pairs = [partner_pairs(count, step * 4**axis) for step in STEPS]
        return [lax.ppermute(state, "seq", pair) for pair in pairs]

    def weighed(decays, first, terms):
        return sum(decays[first + n] * term for n, term in enumerate(terms))

    signal = tiles(key_rows * value_rows)
    state = kernel_call(
        end_state_kernel, f32(*shape), (signal, damping), 2_000_000_000, 600_000
    )
    decays_z, own_z = kernel_call(
        lambda *refs: run_own(0, rows, *refs),
        (f32(7, *shape), f32(*shape)),
        (damping, state),
        1_000_000_000,
        600_000,
    )
    decays_y = kernel_call(
        lambda *refs: run_kernel(1, rows, *refs),
        f32(7, *shape),
        (damping,),
        1_000_000_000,
        600_000,
    )
    near = kernel_call(
        local_kernel, f32(*signal.shape), (signal, damping, gain), 3_000_000_000, 1_000_000
    )
    last, to_run, eight, powers = kernel_call(
        lambda *refs: last_kernel(rows, *refs),
        (f32(3, *shape), f32(2, *shape), f32(*shape), f32(MODES, *shape[1:])),
        (damping, gain),
        1_000_000_000,
        1_000_000,
    )
    from_z = swap(state, 0)
    total_z = own_z + weighed(decays_z, 1, from_z)
    from_y = swap(total_z, 1)
    total_y = weighed(decays_y, 0, [total_z] + from_y)
    from_x = swap(total_y, 2)
    base = to_run[0] * weighed(decays_z, 4, from_z)
    base = base + to_run[1] * weighed(decays_y, 4, from_y)

    parts = 2
    width = out_weight.shape[1] // lax.axis_size("ch")
    piece = f32(rows, width // parts)
    starts = [n * (width // parts) for n in range(parts)]

    gated, first = kernel_call(
        lambda *refs: gate_kernel([(3, 0)], *refs),
        (jax.ShapeDtypeStruct((rows, channels), jnp.bfloat16), piece),
        (queries, near, powers, eight, base, last, *from_x, out_weight),
        1_500_000_000,
        3_000_000,
        (pltpu.VMEM(shape, jnp.float32),),
    )

    def projected(gated, pieces):
        return kernel_call(
            lambda *refs: project_kernel(pieces, *refs),
            (piece,) * len(pieces),
            (gated, out_weight),
            300_000_000 * len(pieces),
            1_000_000 * len(pieces),
        )

    def core_swap(pieces):
        return [lax.ppermute(one, "ch", partner_pairs(4, 1)) for one in pieces]

    def chip_swap(pieces):
        return [lax.ppermute(one, "ch", partner_pairs(4, 2)) for one in pieces]

    (kept,) = projected(gated, [(2, 0)])
    (arrived,) = core_swap([first])
    gated, away = lax.optimization_barrier((gated, kept + arrived))
    second, kept, *sent = projected(
        gated, [(3, starts[1]), (2, starts[1])] + [(g, n) for g in (1, 0) for n in starts]
    )
    arrived, *home = core_swap([second, *sent[:parts]])
    away = chip_swap([away, kept + arrived])
    home = [a + b for a, b in zip(sent[parts:], home)]
    return kernel_call(
        finish_kernel,
        jax.ShapeDtypeStruct((rows, width), jnp.bfloat16),
        (*home, *away),
        1_000_000,
        2_000_000,
    )


def solution(mesh):
    in_specs = (
        P("seq", "ch"),
        P("seq", "ch"),
        P("seq", "ch"),
        P(None, "ch"),
        P(None, "ch"),
        P("ch", None),
    )
    return jax.shard_map(
        local, mesh=mesh, in_specs=in_specs, out_specs=P("seq", "ch"), check_vma=False
    )
```

```python
import jax
import jax.numpy as jnp
from jax import lax
from jax.experimental import pallas as pl
from jax.experimental.pallas import tpu as pltpu
from jax.sharding import PartitionSpec as P

MODES = 16
HALVES = MODES // 8
LANES = 128
SCOPE = 12 * 1024 * 1024
STEPS = (1, 3, 2)
HANDED = 8


def tiles(array):
    rows, columns = array.shape
    cut = array.reshape(rows // 8, 8, columns // LANES, LANES)
    return cut.transpose(0, 2, 1, 3).reshape(rows // 8, 8 * (columns // LANES), LANES)


def spread(values, index):
    return jnp.broadcast_to(values[index : index + 1, :], (8, LANES))


def f32(*shape):
    return jax.ShapeDtypeStruct(shape, jnp.float32)


def kernel_call(body, out_shape, inputs, flops, size, scratch=()):
    outs = jax.tree.map(lambda _: pl.BlockSpec(memory_space=pltpu.VMEM), out_shape)
    return pl.pallas_call(
        body,
        out_shape=out_shape,
        in_specs=[pl.BlockSpec(memory_space=pltpu.VMEM)] * len(inputs),
        out_specs=outs,
        scratch_shapes=scratch,
        cost_estimate=pl.CostEstimate(flops=flops, bytes_accessed=size, transcendentals=0),
        compiler_params=pltpu.CompilerParams(vmem_limit_bytes=SCOPE),
    )(*inputs)


def end_state_kernel(signal_ref, damping_ref, state_ref):
    outer, lanes = signal_ref.shape[0], signal_ref.shape[1] // 8
    place = lax.broadcasted_iota(jnp.int32, (8, LANES), 0)
    for g in range(lanes):
        block = pl.ds(8 * g, 8)
        signal = [signal_ref[i, block, :] for i in range(outer)]
        for half in range(HALVES):
            decay = jnp.exp(-damping_ref[half, block, :])
            result = None
            for m in range(8):
                once = spread(decay, m)
                twice = once * once
                four = twice * twice
                eight = four * four
                total = signal[0]
                for i in range(1, outer):
                    total = eight * total + signal[i]
                total = total + once * pltpu.roll(total, 1, 0)
                total = total + twice * pltpu.roll(total, 2, 0)
                total = total + four * pltpu.roll(total, 4, 0)
                if m != 7:
                    total = pltpu.roll(total, m + 1, 0)
                result = total if result is None else jnp.where(place == m, total, result)
            state_ref[half, block, :] = result


def local_kernel(signal_ref, damping_ref, gain_ref, query_ref, out_ref, handed_ref):
    def row(ref, outer, inner):
        return ref[outer, pl.ds(inner, 8, stride=8), :]

    decay = [jnp.exp(-row(damping_ref, m // 8, m % 8)) for m in range(MODES)]
    gain = [row(gain_ref, m // 8, m % 8) for m in range(MODES)]

    def body(outer, state):
        for inner in range(8):
            signal = row(signal_ref, outer, inner)
            state = tuple(decay[m] * state[m] + signal for m in range(MODES))
            terms = [gain[m] * state[m] for m in range(MODES)]
            while len(terms) > 1:
                terms = [terms[n] + terms[n + 1] for n in range(0, len(terms), 2)]
            out_ref[outer, pl.ds(inner, 8, stride=8), :] = terms[0]
        return state

    zero = jnp.zeros((8, LANES), jnp.float32)
    lax.fori_loop(0, signal_ref.shape[0], body, (zero,) * MODES)
    count = handed_ref.shape[1]
    handed_ref[0] = query_ref[0:count]
    handed_ref[1] = out_ref[0:count]


def places():
    at = lax.axis_index("seq")
    return [lax.rem(at, 4), lax.rem(lax.div(at, 4), 4), lax.div(at, 16)]


def helped(z):
    return lax.rem(z + jnp.where(lax.axis_index("ch") < 2, 3, 1), 4)


def entry_decay(damping, target, there):
    ahead = jnp.maximum(target - there - 1, 0).astype(jnp.float32)
    before = (there < target).astype(jnp.float32)
    return jnp.exp(damping * ahead) * before


def run_kernel(axis, rows, damping_ref, out_ref):
    here = places()[axis]
    damping = damping_ref[...] * (-1.0 * rows * 4**axis)
    for n, step in enumerate((0, *STEPS)):
        there = here ^ step
        out_ref[n] = jnp.exp(damping * (3 - there).astype(jnp.float32))
        if step:
            out_ref[3 + n] = entry_decay(damping, here, there)
        if axis == 0:
            out_ref[7 + n] = entry_decay(damping, helped(here), there)


def run_own(axis, rows, damping_ref, state_ref, out_ref, own_ref):
    run_kernel(axis, rows, damping_ref, out_ref)
    own_ref[...] = out_ref[0] * state_ref[...]


def last_kernel(rows, damping_ref, gain_ref, out_ref, scale_ref, eight_ref, powers_ref):
    z, y, x = places()
    damping, gain = damping_ref[...], gain_ref[...]
    scale_ref[0] = gain
    for n, target in enumerate((z, helped(z))):
        scale_ref[1 + n] = gain * jnp.exp(-damping * (target * rows).astype(jnp.float32))
    to_run = jnp.exp(-damping * (4 * y * rows).astype(jnp.float32))
    for n, step in enumerate(STEPS):
        out_ref[n] = to_run * entry_decay(damping * (-16.0 * rows), x, x ^ step)
    eight_ref[...] = jnp.exp(-8.0 * damping)
    since = 1.0 + lax.broadcasted_iota(jnp.int32, (8, LANES), 0).astype(jnp.float32)
    for g in range(damping.shape[1] // 8):
        for half in range(HALVES):
            part = damping_ref[half, 8 * g : 8 * g + 8, :]
            for m in range(8):
                powers_ref[8 * half + m, 8 * g : 8 * g + 8, :] = jnp.exp(
                    -spread(part, m) * since
                )


def project(gated, weight_ref, group):
    width = weight_ref.shape[1] // 4
    first = pl.multiple_of((lax.axis_index("ch") ^ group) * width, LANES)
    return jnp.dot(
        gated, weight_ref[:, pl.ds(first, width)], preferred_element_type=jnp.float32
    )


def project_away(gated_ref, weight_ref, group, out_ref):
    skipped = gated_ref.shape[0] - out_ref.shape[0]
    out_ref[...] = project(gated_ref[skipped:, :], weight_ref, group)


def gate_kernel(*refs):
    query_ref, local_ref, handed_ref, powers_ref, eight_ref = refs[:5]
    bases, scale_ref, last_ref, arrived, weight_ref = refs[5:7], *refs[7:9], refs[9:12], refs[12]
    gated_ref, sent_ref, state_ref = refs[13:]
    far = sum(last_ref[n] * arrived[n][...] for n in range(3))
    for n in range(2):
        state_ref[n] = bases[n][...] + scale_ref[1 + n] * far
    blocks = ((query_ref, local_ref), (handed_ref.at[0], handed_ref.at[1]))

    def body(g, carry):
        block = pl.ds(pl.multiple_of(8 * g, 8), 8)
        columns = pl.ds(pl.multiple_of(LANES * g, LANES), LANES)
        first = 0
        for n, (queries, locals_) in enumerate(blocks):
            outer = queries.shape[0]
            rows = [locals_[i, block, :] for i in range(outer)]
            for half in range(HALVES):
                entry, eight = state_ref[n, half, block, :], eight_ref[half, block, :]
                for m in range(8):
                    term = spread(entry, m) * powers_ref[8 * half + m, block, :]
                    factor = spread(eight, m)
                    for i in range(outer):
                        rows[i] = rows[i] + term
                        if i + 1 < outer:
                            term = term * factor
            rows = [queries[i, block, :] * rows[i] for i in range(outer)]
            gated_ref[pl.ds(first, 8 * outer), columns] = jnp.concatenate(
                rows, axis=0
            ).astype(jnp.bfloat16)
            first += 8 * outer
        return carry

    lax.fori_loop(0, query_ref.shape[1] // 8, body, 0)
    project_away(gated_ref, weight_ref, 3, sent_ref)


def rest_kernel(gated_ref, weight_ref, kept_ref, sent_ref, home_ref):
    project_away(gated_ref, weight_ref, 2, kept_ref)
    rows = home_ref.shape[0]
    sent_ref[...] = project(gated_ref[:rows, :], weight_ref, 1)
    home_ref[...] = project(gated_ref[:rows, :], weight_ref, 0)


def finish_kernel(home_ref, helped_ref, own_ref, out_ref):
    count = helped_ref.shape[0]
    out_ref[:count, :] = (home_ref[:count, :] + helped_ref[...]).astype(jnp.bfloat16)
    out_ref[count:, :] = (home_ref[count:, :] + own_ref[...]).astype(jnp.bfloat16)


def partner_pairs(size, step):
    return [(i, i ^ step) for i in range(size)]


def along_z(count, turn):
    pairs = []
    for i in range(4 * count):
        z, low = turn((i // 4) % 4, (i // 2) % 2)
        pairs.append((i, i // 16 * 16 + (z % 4) * 4 + low * 2 + i % 2))
    return pairs


def local(value_rows, key_rows, query_rows, pole_weights, damping_speeds, out_weight):
    rows, channels = value_rows.shape
    count = lax.axis_size("seq")
    queries = tiles(query_rows)
    damping = tiles(damping_speeds)
    gain = tiles(pole_weights * jnp.sqrt(-jnp.expm1(-2.0 * damping_speeds)))
    shape = damping.shape

    def swap(state, axis):
        pairs = [partner_pairs(count, step * 4**axis) for step in STEPS]
        return [lax.ppermute(state, "seq", pair) for pair in pairs]

    def run_total(own, decays, arrived):
        near_by, farthest = arrived[:-1], arrived[-1]
        own = lax.optimization_barrier(own + decays[len(arrived)] * farthest)
        return own + weighed(decays, 1, near_by)

    def weighed(decays, first, terms):
        return sum(decays[first + n] * term for n, term in enumerate(terms))

    signal = tiles(key_rows * value_rows)
    state = kernel_call(
        end_state_kernel, f32(*shape), (signal, damping), 2_000_000_000, 600_000
    )
    decays_z, own_z = kernel_call(
        lambda *refs: run_own(0, rows, *refs),
        (f32(11, *shape), f32(*shape)),
        (damping, state),
        1_000_000_000,
        800_000,
    )
    decays_y = kernel_call(
        lambda *refs: run_kernel(1, rows, *refs),
        f32(7, *shape),
        (damping,),
        1_000_000_000,
        600_000,
    )
    near, handed = kernel_call(
        local_kernel,
        (f32(*signal.shape), f32(2, HANDED, *signal.shape[1:])),
        (signal, damping, gain, queries),
        3_000_000_000,
        1_500_000,
    )
    last, scale, eight, powers = kernel_call(
        lambda *refs: last_kernel(rows, *refs),
        (f32(3, *shape), f32(3, *shape), f32(*shape), f32(MODES, *shape[1:])),
        (damping, gain),
        1_000_000_000,
        1_000_000,
    )
    from_z = swap(state, 0)
    total_z = run_total(own_z, decays_z, from_z)
    total_z, _ = lax.optimization_barrier((total_z, handed))
    handed = lax.ppermute(
        handed, ("seq", "ch"), along_z(count, lambda z, low: (z + 1 - 2 * low, low))
    )
    from_y = swap(total_z, 1)
    total_y = run_total(decays_y[0] * total_z, decays_y, from_y)
    from_x = swap(total_y, 2)
    from_runs = weighed(decays_y, 4, from_y)
    bases = [
        scale[0] * weighed(decays_z, 4, from_z) + scale[1] * from_runs,
        scale[0] * weighed(decays_z, 7, [state] + from_z) + scale[2] * from_runs,
    ]

    width = out_weight.shape[1] // lax.axis_size("ch")
    whole = f32(rows, width)
    gated, sent = kernel_call(
        gate_kernel,
        (jax.ShapeDtypeStruct((rows + 8 * HANDED, channels), jnp.bfloat16), whole),
        (
            queries,
            near,
            handed,
            powers,
            eight,
            *bases,
            scale,
            last,
            *from_x,
            out_weight,
        ),
        2_000_000_000,
        3_000_000,
        (pltpu.VMEM((2, *shape), jnp.float32),),
    )
    kept, home_sent, home_kept = kernel_call(
        rest_kernel, (whole,) * 3, (gated, out_weight), 1_500_000_000, 2_000_000
    )

    def core_swap(one):
        return lax.ppermute(one, "ch", partner_pairs(4, 1))

    away = kept + core_swap(sent)
    away, home_sent = lax.optimization_barrier((away, home_sent))
    cut = rows - 8 * HANDED
    helped_away = lax.ppermute(
        away[cut:],
        ("seq", "ch"),
        along_z(count, lambda z, low: (z - 1 + 2 * low, 1 - low)),
    )
    own_away = lax.ppermute(away[:cut], "ch", partner_pairs(4, 2))
    home = home_kept + core_swap(home_sent)
    return kernel_call(
        finish_kernel,
        jax.ShapeDtypeStruct((rows, width), jnp.bfloat16),
        (home, helped_away, own_away),
        1_000_000,
        2_000_000,
    )


def solution(mesh):
    in_specs = (
        P("seq", "ch"),
        P("seq", "ch"),
        P("seq", "ch"),
        P(None, "ch"),
        P(None, "ch"),
        P("ch", None),
    )
    return jax.shard_map(
        local, mesh=mesh, in_specs=in_specs, out_specs=P("seq", "ch"), check_vma=False
    )
```

```python
import jax
import jax.numpy as jnp
from jax import lax
from jax.experimental import pallas as pl
from jax.experimental.pallas import tpu as pltpu
from jax.sharding import PartitionSpec as P

MODES = 16
HALVES = MODES // 8
LANES = 128
SCOPE = 12 * 1024 * 1024
STEPS = (1, 3, 2)
HANDED = 8


def tiles(array):
    rows, columns = array.shape
    cut = array.reshape(rows // 8, 8, columns // LANES, LANES)
    return cut.transpose(0, 2, 1, 3).reshape(rows // 8, 8 * (columns // LANES), LANES)


def spread(values, index):
    return jnp.broadcast_to(values[index : index + 1, :], (8, LANES))


def f32(*shape):
    return jax.ShapeDtypeStruct(shape, jnp.float32)


def kernel_call(body, out_shape, inputs, flops, size, scratch=()):
    outs = jax.tree.map(lambda _: pl.BlockSpec(memory_space=pltpu.VMEM), out_shape)
    return pl.pallas_call(
        body,
        out_shape=out_shape,
        in_specs=[pl.BlockSpec(memory_space=pltpu.VMEM)] * len(inputs),
        out_specs=outs,
        scratch_shapes=scratch,
        cost_estimate=pl.CostEstimate(flops=flops, bytes_accessed=size, transcendentals=0),
        compiler_params=pltpu.CompilerParams(vmem_limit_bytes=SCOPE),
    )(*inputs)


def split(stacked_ref):
    outer = stacked_ref.shape[0] - HALVES
    return stacked_ref.at[pl.ds(0, outer)], stacked_ref.at[pl.ds(outer, HALVES)]


def end_state_kernel(stacked_ref, state_ref):
    signal_ref, damping_ref = split(stacked_ref)
    outer, lanes = signal_ref.shape[0], signal_ref.shape[1] // 8
    place = lax.broadcasted_iota(jnp.int32, (8, LANES), 0)
    for g in range(lanes):
        block = pl.ds(8 * g, 8)
        signal = [signal_ref[i, block, :] for i in range(outer)]
        for half in range(HALVES):
            decay = jnp.exp(-damping_ref[half, block, :])
            result = None
            for m in range(8):
                once = spread(decay, m)
                twice = once * once
                four = twice * twice
                eight = four * four
                total = signal[0]
                for i in range(1, outer):
                    total = eight * total + signal[i]
                total = total + once * pltpu.roll(total, 1, 0)
                total = total + twice * pltpu.roll(total, 2, 0)
                total = total + four * pltpu.roll(total, 4, 0)
                if m != 7:
                    total = pltpu.roll(total, m + 1, 0)
                result = total if result is None else jnp.where(place == m, total, result)
            state_ref[half, block, :] = result


def local_kernel(stacked_ref, gain_ref, query_ref, out_ref, handed_ref):
    signal_ref, damping_ref = split(stacked_ref)

    def row(ref, outer, inner):
        return ref[outer, pl.ds(inner, 8, stride=8), :]

    decay = [jnp.exp(-row(damping_ref, m // 8, m % 8)) for m in range(MODES)]
    gain = [row(gain_ref, m // 8, m % 8) for m in range(MODES)]

    def body(outer, state):
        for inner in range(8):
            signal = row(signal_ref, outer, inner)
            state = tuple(decay[m] * state[m] + signal for m in range(MODES))
            terms = [gain[m] * state[m] for m in range(MODES)]
            while len(terms) > 1:
                terms = [terms[n] + terms[n + 1] for n in range(0, len(terms), 2)]
            out_ref[outer, pl.ds(inner, 8, stride=8), :] = terms[0]
        return state

    zero = jnp.zeros((8, LANES), jnp.float32)
    lax.fori_loop(0, signal_ref.shape[0], body, (zero,) * MODES)
    count = handed_ref.shape[1]
    handed_ref[0] = query_ref[0:count]
    handed_ref[1] = out_ref[0:count]


def places():
    at = lax.axis_index("seq")
    return [lax.rem(at, 4), lax.rem(lax.div(at, 4), 4), lax.div(at, 16)]


def helped(z):
    return lax.rem(z + jnp.where(lax.axis_index("ch") < 2, 3, 1), 4)


def entry_decay(damping, target, there):
    ahead = jnp.maximum(target - there - 1, 0).astype(jnp.float32)
    before = (there < target).astype(jnp.float32)
    return jnp.exp(damping * ahead) * before


def run_kernel(axis, rows, stacked_ref, out_ref):
    here = places()[axis]
    damping = split(stacked_ref)[1][...] * (-1.0 * rows * 4**axis)
    for n, step in enumerate((0, *STEPS)):
        there = here ^ step
        out_ref[n] = jnp.exp(damping * (3 - there).astype(jnp.float32))
        if step:
            out_ref[3 + n] = entry_decay(damping, here, there)
        if axis == 0:
            out_ref[7 + n] = entry_decay(damping, helped(here), there)


def run_own(axis, rows, stacked_ref, state_ref, out_ref, own_ref):
    run_kernel(axis, rows, stacked_ref, out_ref)
    own_ref[...] = out_ref[0] * state_ref[...]


def last_kernel(rows, stacked_ref, gain_ref, out_ref, scale_ref, eight_ref, powers_ref):
    z, y, x = places()
    damping_ref = split(stacked_ref)[1]
    damping, gain = damping_ref[...], gain_ref[...]
    scale_ref[0] = gain
    for n, target in enumerate((z, helped(z))):
        scale_ref[1 + n] = gain * jnp.exp(-damping * (target * rows).astype(jnp.float32))
    to_run = jnp.exp(-damping * (4 * y * rows).astype(jnp.float32))
    for n, step in enumerate(STEPS):
        out_ref[n] = to_run * entry_decay(damping * (-16.0 * rows), x, x ^ step)
    eight_ref[...] = jnp.exp(-8.0 * damping)
    since = 1.0 + lax.broadcasted_iota(jnp.int32, (8, LANES), 0).astype(jnp.float32)
    for g in range(damping.shape[1] // 8):
        for half in range(HALVES):
            part = damping_ref[half, 8 * g : 8 * g + 8, :]
            for m in range(8):
                powers_ref[8 * half + m, 8 * g : 8 * g + 8, :] = jnp.exp(
                    -spread(part, m) * since
                )


def project(gated, weight_ref, group):
    width = weight_ref.shape[1] // 4
    first = pl.multiple_of((lax.axis_index("ch") ^ group) * width, LANES)
    return jnp.dot(
        gated, weight_ref[:, pl.ds(first, width)], preferred_element_type=jnp.float32
    )


def project_away(gated_ref, weight_ref, group, own_ref, helped_ref):
    rows = own_ref.shape[0] + helped_ref.shape[0]
    skipped = gated_ref.shape[0] - rows
    result = project(gated_ref[skipped:, :], weight_ref, group)
    own_ref[...] = result[: own_ref.shape[0]]
    helped_ref[...] = result[own_ref.shape[0] :]


def gate_kernel(*refs):
    query_ref, local_ref, handed_ref, powers_ref, eight_ref = refs[:5]
    bases, scale_ref, last_ref, arrived, weight_ref = refs[5:7], *refs[7:9], refs[9:12], refs[12]
    gated_ref, own_ref, helped_ref, state_ref = refs[13:]
    far = sum(last_ref[n] * arrived[n][...] for n in range(3))
    for n in range(2):
        state_ref[n] = bases[n][...] + scale_ref[1 + n] * far
    blocks = ((query_ref, local_ref), (handed_ref.at[0], handed_ref.at[1]))

    def body(g, carry):
        block = pl.ds(pl.multiple_of(8 * g, 8), 8)
        columns = pl.ds(pl.multiple_of(LANES * g, LANES), LANES)
        first = 0
        for n, (queries, locals_) in enumerate(blocks):
            outer = queries.shape[0]
            rows = [locals_[i, block, :] for i in range(outer)]
            for half in range(HALVES):
                entry, eight = state_ref[n, half, block, :], eight_ref[half, block, :]
                for m in range(8):
                    term = spread(entry, m) * powers_ref[8 * half + m, block, :]
                    factor = spread(eight, m)
                    for i in range(outer):
                        rows[i] = rows[i] + term
                        if i + 1 < outer:
                            term = term * factor
            rows = [queries[i, block, :] * rows[i] for i in range(outer)]
            gated_ref[pl.ds(first, 8 * outer), columns] = jnp.concatenate(
                rows, axis=0
            ).astype(jnp.bfloat16)
            first += 8 * outer
        return carry

    lax.fori_loop(0, query_ref.shape[1] // 8, body, 0)
    project_away(gated_ref, weight_ref, 3, own_ref, helped_ref)


def rest_kernel(gated_ref, weight_ref, own_ref, helped_ref, sent_ref, home_ref):
    project_away(gated_ref, weight_ref, 2, own_ref, helped_ref)
    rows = home_ref.shape[0]
    sent_ref[...] = project(gated_ref[:rows, :], weight_ref, 1)
    home_ref[...] = project(gated_ref[:rows, :], weight_ref, 0)


def finish_kernel(home_ref, helped_ref, own_ref, core_ref, out_ref):
    count = helped_ref.shape[0]
    for part, away_ref in ((pl.ds(0, count), helped_ref), (pl.ds(count, own_ref.shape[0]), own_ref)):
        total = core_ref[part, :] + home_ref[part, :] + away_ref[...]
        out_ref[part, :] = total.astype(jnp.bfloat16)


def partner_pairs(size, step):
    return [(i, i ^ step) for i in range(size)]


def along_z(count, turn):
    pairs = []
    for i in range(4 * count):
        z, low = turn((i // 4) % 4, (i // 2) % 2)
        pairs.append((i, i // 16 * 16 + (z % 4) * 4 + low * 2 + i % 2))
    return pairs


def local(value_rows, key_rows, query_rows, pole_weights, damping_speeds, out_weight):
    rows, channels = value_rows.shape
    count = lax.axis_size("seq")
    queries = tiles(query_rows)
    more, below = ((0, MODES, 0), (0, 0, 0)), ((rows, 0, 0), (0, 0, 0))
    keys, values = (lax.pad(one, 0.0, more) for one in (key_rows, value_rows))
    stacked = tiles(keys * values + lax.pad(damping_speeds, 0.0, below))
    gain = tiles(pole_weights * jnp.sqrt(-jnp.expm1(-2.0 * damping_speeds)))
    shape = gain.shape

    def swap(state, axis):
        pairs = [partner_pairs(count, step * 4**axis) for step in STEPS]
        return [lax.ppermute(state, "seq", pair) for pair in pairs]

    def run_total(own, decays, arrived):
        near_by, farthest = arrived[:-1], arrived[-1]
        own = lax.optimization_barrier(own + decays[len(arrived)] * farthest)
        return own + weighed(decays, 1, near_by)

    def weighed(decays, first, terms):
        return sum(decays[first + n] * term for n, term in enumerate(terms))

    state = kernel_call(
        end_state_kernel, f32(*shape), (stacked,), 2_000_000_000, 600_000
    )
    decays_z, own_z = kernel_call(
        lambda *refs: run_own(0, rows, *refs),
        (f32(11, *shape), f32(*shape)),
        (stacked, state),
        1_000_000_000,
        800_000,
    )
    decays_y = kernel_call(
        lambda *refs: run_kernel(1, rows, *refs),
        f32(7, *shape),
        (stacked,),
        1_000_000_000,
        600_000,
    )
    near, handed = kernel_call(
        local_kernel,
        (f32(*queries.shape), f32(2, HANDED, *queries.shape[1:])),
        (stacked, gain, queries),
        3_000_000_000,
        1_500_000,
    )
    last, scale, eight, powers = kernel_call(
        lambda *refs: last_kernel(rows, *refs),
        (f32(3, *shape), f32(3, *shape), f32(*shape), f32(MODES, *shape[1:])),
        (stacked, gain),
        1_000_000_000,
        1_000_000,
    )
    from_z = swap(state, 0)
    total_z = run_total(own_z, decays_z, from_z)
    total_z, _ = lax.optimization_barrier((total_z, handed))
    handed = lax.ppermute(
        handed, ("seq", "ch"), along_z(count, lambda z, low: (z + 1 - 2 * low, low))
    )
    from_y = swap(total_z, 1)
    total_y = run_total(decays_y[0] * total_z, decays_y, from_y)
    from_x = swap(total_y, 2)
    from_runs = weighed(decays_y, 4, from_y)
    bases = [
        scale[0] * weighed(decays_z, 4, from_z) + scale[1] * from_runs,
        scale[0] * weighed(decays_z, 7, [state] + from_z) + scale[2] * from_runs,
    ]

    width = out_weight.shape[1] // lax.axis_size("ch")
    whole = f32(rows, width)
    away = (f32(rows - 8 * HANDED, width), f32(8 * HANDED, width))
    gated, own_sent, helped_sent = kernel_call(
        gate_kernel,
        (jax.ShapeDtypeStruct((rows + 8 * HANDED, channels), jnp.bfloat16), *away),
        (
            queries,
            near,
            handed,
            powers,
            eight,
            *bases,
            scale,
            last,
            *from_x,
            out_weight,
        ),
        2_000_000_000,
        3_000_000,
        (pltpu.VMEM((2, *shape), jnp.float32),),
    )
    own_kept, helped_kept, home_sent, home_kept = kernel_call(
        rest_kernel, (*away, whole, whole), (gated, out_weight), 1_000_000, 10_000
    )

    def core_swap(one):
        return lax.ppermute(one, "ch", partner_pairs(4, 1))

    own_away = own_kept + core_swap(own_sent)
    own_away, home_sent = lax.optimization_barrier((own_away, home_sent))
    helped_away = helped_kept + core_swap(helped_sent)
    helped_away = lax.ppermute(
        helped_away,
        ("seq", "ch"),
        along_z(count, lambda z, low: (z - 1 + 2 * low, 1 - low)),
    )
    own_away = lax.ppermute(own_away, "ch", partner_pairs(4, 2))
    return kernel_call(
        finish_kernel,
        jax.ShapeDtypeStruct((rows, width), jnp.bfloat16),
        (home_kept, helped_away, own_away, core_swap(home_sent)),
        1_000_000,
        2_000_000,
    )


def solution(mesh):
    in_specs = (
        P("seq", "ch"),
        P("seq", "ch"),
        P("seq", "ch"),
        P(None, "ch"),
        P(None, "ch"),
        P("ch", None),
    )
    return jax.shard_map(
        local, mesh=mesh, in_specs=in_specs, out_specs=P("seq", "ch"), check_vma=False
    )
```

```python
import jax
import jax.numpy as jnp
from jax import lax
from jax.experimental import pallas as pl
from jax.experimental.pallas import tpu as pltpu
from jax.sharding import PartitionSpec as P

MODES = 16
HALVES = MODES // 8
LANES = 128
SCOPE = 12 * 1024 * 1024
STEPS = (1, 3, 2)
HANDED = 8


def tiles(array):
    rows, columns = array.shape
    cut = array.reshape(rows // 8, 8, columns // LANES, LANES)
    return cut.transpose(0, 2, 1, 3).reshape(rows // 8, 8 * (columns // LANES), LANES)


def spread(values, index):
    return jnp.broadcast_to(values[index : index + 1, :], (8, LANES))


def f32(*shape):
    return jax.ShapeDtypeStruct(shape, jnp.float32)


def kernel_call(body, out_shape, inputs, flops, size, scratch=()):
    outs = jax.tree.map(lambda _: pl.BlockSpec(memory_space=pltpu.VMEM), out_shape)
    return pl.pallas_call(
        body,
        out_shape=out_shape,
        in_specs=[pl.BlockSpec(memory_space=pltpu.VMEM)] * len(inputs),
        out_specs=outs,
        scratch_shapes=scratch,
        cost_estimate=pl.CostEstimate(flops=flops, bytes_accessed=size, transcendentals=0),
        compiler_params=pltpu.CompilerParams(vmem_limit_bytes=SCOPE),
    )(*inputs)


def split(stacked_ref):
    outer = stacked_ref.shape[0] - HALVES
    return stacked_ref.at[pl.ds(0, outer)], stacked_ref.at[pl.ds(outer, HALVES)]


def end_state_kernel(stacked_ref, state_ref):
    signal_ref, damping_ref = split(stacked_ref)
    outer, lanes = signal_ref.shape[0], signal_ref.shape[1] // 8
    place = lax.broadcasted_iota(jnp.int32, (8, LANES), 0)
    for g in range(lanes):
        block = pl.ds(8 * g, 8)
        signal = [signal_ref[i, block, :] for i in range(outer)]
        for half in range(HALVES):
            decay = jnp.exp(-damping_ref[half, block, :])
            result = None
            for m in range(8):
                once = spread(decay, m)
                twice = once * once
                four = twice * twice
                eight = four * four
                total = signal[0]
                for i in range(1, outer):
                    total = eight * total + signal[i]
                total = total + once * pltpu.roll(total, 1, 0)
                total = total + twice * pltpu.roll(total, 2, 0)
                total = total + four * pltpu.roll(total, 4, 0)
                if m != 7:
                    total = pltpu.roll(total, m + 1, 0)
                result = total if result is None else jnp.where(place == m, total, result)
            state_ref[half, block, :] = result


def local_kernel(stacked_ref, gain_ref, query_ref, out_ref, handed_ref):
    signal_ref, damping_ref = split(stacked_ref)

    def row(ref, outer, inner):
        return ref[outer, pl.ds(inner, 8, stride=8), :]

    decay = [jnp.exp(-row(damping_ref, m // 8, m % 8)) for m in range(MODES)]
    gain = [row(gain_ref, m // 8, m % 8) for m in range(MODES)]

    def body(outer, state):
        for inner in range(8):
            signal = row(signal_ref, outer, inner)
            state = tuple(decay[m] * state[m] + signal for m in range(MODES))
            terms = [gain[m] * state[m] for m in range(MODES)]
            while len(terms) > 1:
                terms = [terms[n] + terms[n + 1] for n in range(0, len(terms), 2)]
            out_ref[outer, pl.ds(inner, 8, stride=8), :] = terms[0]
        return state

    zero = jnp.zeros((8, LANES), jnp.float32)
    lax.fori_loop(0, signal_ref.shape[0], body, (zero,) * MODES)
    count = handed_ref.shape[1]
    handed_ref[0] = query_ref[0:count]
    handed_ref[1] = out_ref[0:count]


def places():
    at = lax.axis_index("seq")
    return [lax.rem(at, 4), lax.rem(lax.div(at, 4), 4), lax.div(at, 16)]


def helped(z):
    return lax.rem(z + jnp.where(lax.axis_index("ch") < 2, 3, 1), 4)


def entry_decay(damping, target, there):
    ahead = jnp.maximum(target - there - 1, 0).astype(jnp.float32)
    before = (there < target).astype(jnp.float32)
    return jnp.exp(damping * ahead) * before


def run_kernel(axis, rows, stacked_ref, out_ref):
    here = places()[axis]
    damping = split(stacked_ref)[1][...] * (-1.0 * rows * 4**axis)
    for n, step in enumerate((0, *STEPS)):
        there = here ^ step
        out_ref[n] = jnp.exp(damping * (3 - there).astype(jnp.float32))
        if step:
            out_ref[3 + n] = entry_decay(damping, here, there)
        if axis == 0:
            out_ref[7 + n] = entry_decay(damping, helped(here), there)


def run_own(axis, rows, stacked_ref, state_ref, out_ref, own_ref):
    run_kernel(axis, rows, stacked_ref, out_ref)
    own_ref[...] = out_ref[0] * state_ref[...]


def last_kernel(rows, stacked_ref, gain_ref, out_ref, scale_ref, eight_ref, powers_ref):
    z, y, x = places()
    damping_ref = split(stacked_ref)[1]
    damping, gain = damping_ref[...], gain_ref[...]
    scale_ref[0] = gain
    for n, target in enumerate((z, helped(z))):
        scale_ref[1 + n] = gain * jnp.exp(-damping * (target * rows).astype(jnp.float32))
    to_run = jnp.exp(-damping * (4 * y * rows).astype(jnp.float32))
    for n, step in enumerate(STEPS):
        out_ref[n] = to_run * entry_decay(damping * (-16.0 * rows), x, x ^ step)
    eight_ref[...] = jnp.exp(-8.0 * damping)
    since = 1.0 + lax.broadcasted_iota(jnp.int32, (8, LANES), 0).astype(jnp.float32)
    for g in range(damping.shape[1] // 8):
        for half in range(HALVES):
            part = damping_ref[half, 8 * g : 8 * g + 8, :]
            for m in range(8):
                powers_ref[8 * half + m, 8 * g : 8 * g + 8, :] = jnp.exp(
                    -spread(part, m) * since
                )


def project(gated, weight_ref, group):
    width = weight_ref.shape[1] // 4
    first = pl.multiple_of((lax.axis_index("ch") ^ group) * width, LANES)
    return jnp.dot(
        gated, weight_ref[:, pl.ds(first, width)], preferred_element_type=jnp.float32
    )


def project_away(gated_ref, weight_ref, group, own_ref, helped_ref):
    rows = own_ref.shape[0] + helped_ref.shape[0]
    skipped = gated_ref.shape[0] - rows
    result = project(gated_ref[skipped:, :], weight_ref, group)
    own_ref[...] = result[: own_ref.shape[0]]
    helped_ref[...] = result[own_ref.shape[0] :]


def gate_kernel(*refs):
    query_ref, local_ref, handed_ref, powers_ref, eight_ref = refs[:5]
    bases, scale_ref, last_ref, arrived, weight_ref = refs[5:7], *refs[7:9], refs[9:12], refs[12]
    gated_ref, own_ref, helped_ref, state_ref = refs[13:]
    far = sum(last_ref[n] * arrived[n][...] for n in range(3))
    for n in range(2):
        state_ref[n] = bases[n][...] + scale_ref[1 + n] * far
    blocks = ((query_ref, local_ref), (handed_ref.at[0], handed_ref.at[1]))

    def body(g, carry):
        block = pl.ds(pl.multiple_of(8 * g, 8), 8)
        columns = pl.ds(pl.multiple_of(LANES * g, LANES), LANES)
        sums = [
            [locals_[i, block, :] for i in range(locals_.shape[0])] for _, locals_ in blocks
        ]
        for half in range(HALVES):
            eight = eight_ref[half, block, :]
            entries = [state_ref[n, half, block, :] for n in range(2)]
            for m in range(8):
                power, factor = powers_ref[8 * half + m, block, :], spread(eight, m)
                for rows, entry in zip(sums, entries):
                    term = spread(entry, m) * power
                    for i in range(len(rows)):
                        rows[i] = rows[i] + term
                        if i + 1 < len(rows):
                            term = term * factor
        gated = [
            queries[i, block, :] * rows[i]
            for (queries, _), rows in zip(blocks, sums)
            for i in range(len(rows))
        ]
        gated_ref[:, columns] = jnp.concatenate(gated, axis=0).astype(jnp.bfloat16)
        return carry

    lax.fori_loop(0, query_ref.shape[1] // 8, body, 0, unroll=2)
    project_away(gated_ref, weight_ref, 3, own_ref, helped_ref)


def rest_kernel(gated_ref, weight_ref, own_ref, helped_ref, sent_ref, home_ref):
    project_away(gated_ref, weight_ref, 2, own_ref, helped_ref)
    rows = home_ref.shape[0]
    sent_ref[...] = project(gated_ref[:rows, :], weight_ref, 1)
    home_ref[...] = project(gated_ref[:rows, :], weight_ref, 0)


def finish_kernel(home_ref, helped_ref, own_ref, core_ref, out_ref):
    count = helped_ref.shape[0]
    for part, away_ref in ((pl.ds(0, count), helped_ref), (pl.ds(count, own_ref.shape[0]), own_ref)):
        total = core_ref[part, :] + home_ref[part, :] + away_ref[...]
        out_ref[part, :] = total.astype(jnp.bfloat16)


def partner_pairs(size, step):
    return [(i, i ^ step) for i in range(size)]


def along_z(count, turn):
    pairs = []
    for i in range(4 * count):
        z, low = turn((i // 4) % 4, (i // 2) % 2)
        pairs.append((i, i // 16 * 16 + (z % 4) * 4 + low * 2 + i % 2))
    return pairs


def local(value_rows, key_rows, query_rows, pole_weights, damping_speeds, out_weight):
    rows, channels = value_rows.shape
    count = lax.axis_size("seq")
    queries = tiles(query_rows)
    more, below = ((0, MODES, 0), (0, 0, 0)), ((rows, 0, 0), (0, 0, 0))
    keys, values = (lax.pad(one, 0.0, more) for one in (key_rows, value_rows))
    stacked = tiles(keys * values + lax.pad(damping_speeds, 0.0, below))
    gain = tiles(pole_weights * jnp.sqrt(-jnp.expm1(-2.0 * damping_speeds)))
    shape = gain.shape

    def swap(state, axis):
        pairs = [partner_pairs(count, step * 4**axis) for step in STEPS]
        return [lax.ppermute(state, "seq", pair) for pair in pairs]

    def run_total(own, decays, arrived):
        near_by, farthest = arrived[:-1], arrived[-1]
        own = lax.optimization_barrier(own + decays[len(arrived)] * farthest)
        return own + weighed(decays, 1, near_by)

    def weighed(decays, first, terms):
        return sum(decays[first + n] * term for n, term in enumerate(terms))

    state = kernel_call(
        end_state_kernel, f32(*shape), (stacked,), 2_000_000_000, 600_000
    )
    decays_z, own_z = kernel_call(
        lambda *refs: run_own(0, rows, *refs),
        (f32(11, *shape), f32(*shape)),
        (stacked, state),
        1_000_000_000,
        800_000,
    )
    decays_y = kernel_call(
        lambda *refs: run_kernel(1, rows, *refs),
        f32(7, *shape),
        (stacked,),
        1_000_000_000,
        600_000,
    )
    near, handed = kernel_call(
        local_kernel,
        (f32(*queries.shape), f32(2, HANDED, *queries.shape[1:])),
        (stacked, gain, queries),
        3_000_000_000,
        1_500_000,
    )
    last, scale, eight, powers = kernel_call(
        lambda *refs: last_kernel(rows, *refs),
        (f32(3, *shape), f32(3, *shape), f32(*shape), f32(MODES, *shape[1:])),
        (stacked, gain),
        1_000_000_000,
        1_000_000,
    )
    from_z = swap(state, 0)
    total_z = run_total(own_z, decays_z, from_z)
    total_z, *_ = lax.optimization_barrier((total_z, handed, powers))
    handed = lax.ppermute(
        handed, ("seq", "ch"), along_z(count, lambda z, low: (z + 1 - 2 * low, low))
    )
    from_y = swap(total_z, 1)
    total_y = run_total(decays_y[0] * total_z, decays_y, from_y)
    from_x = swap(total_y, 2)
    from_runs = weighed(decays_y, 4, from_y)
    bases = [
        scale[0] * weighed(decays_z, 4, from_z) + scale[1] * from_runs,
        scale[0] * weighed(decays_z, 7, [state] + from_z) + scale[2] * from_runs,
    ]

    width = out_weight.shape[1] // lax.axis_size("ch")
    whole = f32(rows, width)
    away = (f32(rows - 8 * HANDED, width), f32(8 * HANDED, width))
    gated, own_sent, helped_sent = kernel_call(
        gate_kernel,
        (jax.ShapeDtypeStruct((rows + 8 * HANDED, channels), jnp.bfloat16), *away),
        (
            queries,
            near,
            handed,
            powers,
            eight,
            *bases,
            scale,
            last,
            *from_x,
            out_weight,
        ),
        2_000_000_000,
        3_000_000,
        (pltpu.VMEM((2, *shape), jnp.float32),),
    )
    own_kept, helped_kept, home_sent, home_kept = kernel_call(
        rest_kernel, (*away, whole, whole), (gated, out_weight), 1_000_000, 10_000
    )

    def core_swap(one):
        return lax.ppermute(one, "ch", partner_pairs(4, 1))

    own_away = own_kept + core_swap(own_sent)
    own_away, home_sent = lax.optimization_barrier((own_away, home_sent))
    helped_away = helped_kept + core_swap(helped_sent)
    helped_away = lax.ppermute(
        helped_away,
        ("seq", "ch"),
        along_z(count, lambda z, low: (z - 1 + 2 * low, 1 - low)),
    )
    own_away = lax.ppermute(own_away, "ch", partner_pairs(4, 2))
    return kernel_call(
        finish_kernel,
        jax.ShapeDtypeStruct((rows, width), jnp.bfloat16),
        (home_kept, helped_away, own_away, core_swap(home_sent)),
        1_000_000,
        2_000_000,
    )


def solution(mesh):
    in_specs = (
        P("seq", "ch"),
        P("seq", "ch"),
        P("seq", "ch"),
        P(None, "ch"),
        P(None, "ch"),
        P("ch", None),
    )
    return jax.shard_map(
        local, mesh=mesh, in_specs=in_specs, out_specs=P("seq", "ch"), check_vma=False
    )
```

```python
import jax
import jax.numpy as jnp
from jax import lax
from jax.experimental import pallas as pl
from jax.experimental.pallas import tpu as pltpu
from jax.sharding import PartitionSpec as P

MODES = 16
HALVES = MODES // 8
LANES = 128
SCOPE = 12 * 1024 * 1024
STEPS = (1, 3, 2)
HANDED = 8


def tiles(array):
    rows, columns = array.shape
    cut = array.reshape(rows // 8, 8, columns // LANES, LANES)
    return cut.transpose(0, 2, 1, 3).reshape(rows // 8, 8 * (columns // LANES), LANES)


def spread(values, index):
    return jnp.broadcast_to(values[index : index + 1, :], (8, LANES))


def f32(*shape):
    return jax.ShapeDtypeStruct(shape, jnp.float32)


def kernel_call(body, out_shape, inputs, flops, size, scratch=()):
    outs = jax.tree.map(lambda _: pl.BlockSpec(memory_space=pltpu.VMEM), out_shape)
    return pl.pallas_call(
        body,
        out_shape=out_shape,
        in_specs=[pl.BlockSpec(memory_space=pltpu.VMEM)] * len(inputs),
        out_specs=outs,
        scratch_shapes=scratch,
        cost_estimate=pl.CostEstimate(flops=flops, bytes_accessed=size, transcendentals=0),
        compiler_params=pltpu.CompilerParams(vmem_limit_bytes=SCOPE),
    )(*inputs)


def split(stacked_ref):
    outer = stacked_ref.shape[0] - HALVES
    return stacked_ref.at[pl.ds(0, outer)], stacked_ref.at[pl.ds(outer, HALVES)]


def end_state_kernel(stacked_ref, state_ref):
    signal_ref, damping_ref = split(stacked_ref)
    outer, lanes = signal_ref.shape[0], signal_ref.shape[1] // 8
    place = lax.broadcasted_iota(jnp.int32, (8, LANES), 0)
    for g in range(lanes):
        block = pl.ds(8 * g, 8)
        signal = [signal_ref[i, block, :] for i in range(outer)]
        for half in range(HALVES):
            decay = jnp.exp(-damping_ref[half, block, :])
            result = None
            for m in range(8):
                once = spread(decay, m)
                twice = once * once
                four = twice * twice
                eight = four * four
                total = signal[0]
                for i in range(1, outer):
                    total = eight * total + signal[i]
                total = total + once * pltpu.roll(total, 1, 0)
                total = total + twice * pltpu.roll(total, 2, 0)
                total = total + four * pltpu.roll(total, 4, 0)
                if m != 7:
                    total = pltpu.roll(total, m + 1, 0)
                result = total if result is None else jnp.where(place == m, total, result)
            state_ref[half, block, :] = result


def local_kernel(stacked_ref, gain_ref, query_ref, out_ref, handed_ref):
    signal_ref, damping_ref = split(stacked_ref)

    def row(ref, outer, inner):
        return ref[outer, pl.ds(inner, 8, stride=8), :]

    decay = [jnp.exp(-row(damping_ref, m // 8, m % 8)) for m in range(MODES)]
    gain = [row(gain_ref, m // 8, m % 8) for m in range(MODES)]

    def body(outer, state):
        for inner in range(8):
            signal = row(signal_ref, outer, inner)
            state = tuple(decay[m] * state[m] + signal for m in range(MODES))
            terms = [gain[m] * state[m] for m in range(MODES)]
            while len(terms) > 1:
                terms = [terms[n] + terms[n + 1] for n in range(0, len(terms), 2)]
            out_ref[outer, pl.ds(inner, 8, stride=8), :] = terms[0]
        return state

    zero = jnp.zeros((8, LANES), jnp.float32)
    lax.fori_loop(0, signal_ref.shape[0], body, (zero,) * MODES)
    count = handed_ref.shape[1]
    handed_ref[0] = query_ref[0:count]
    handed_ref[1] = out_ref[0:count]


def places():
    at = lax.axis_index("seq")
    return [lax.rem(at, 4), lax.rem(lax.div(at, 4), 4), lax.div(at, 16)]


def helped(z):
    return lax.rem(z + jnp.where(lax.axis_index("ch") < 2, 3, 1), 4)


def entry_decay(damping, target, there):
    ahead = jnp.maximum(target - there - 1, 0).astype(jnp.float32)
    before = (there < target).astype(jnp.float32)
    return jnp.exp(damping * ahead) * before


def run_kernel(axis, rows, stacked_ref, out_ref):
    here = places()[axis]
    damping = split(stacked_ref)[1][...] * (-1.0 * rows * 4**axis)
    for n, step in enumerate((0, *STEPS)):
        there = here ^ step
        out_ref[n] = jnp.exp(damping * (3 - there).astype(jnp.float32))
        if step:
            out_ref[3 + n] = entry_decay(damping, here, there)
        if axis == 0:
            out_ref[7 + n] = entry_decay(damping, helped(here), there)


def run_own(axis, rows, stacked_ref, state_ref, out_ref, own_ref):
    run_kernel(axis, rows, stacked_ref, out_ref)
    own_ref[...] = out_ref[0] * state_ref[...]


def last_kernel(rows, stacked_ref, gain_ref, out_ref, scale_ref, eight_ref, powers_ref):
    z, y, x = places()
    damping_ref = split(stacked_ref)[1]
    damping, gain = damping_ref[...], gain_ref[...]
    scale_ref[0] = gain
    for n, target in enumerate((z, helped(z))):
        scale_ref[1 + n] = gain * jnp.exp(-damping * (target * rows).astype(jnp.float32))
    to_run = jnp.exp(-damping * (4 * y * rows).astype(jnp.float32))
    for n, step in enumerate(STEPS):
        out_ref[n] = to_run * entry_decay(damping * (-16.0 * rows), x, x ^ step)
    eight_ref[...] = jnp.exp(-8.0 * damping)
    since = 1.0 + lax.broadcasted_iota(jnp.int32, (8, LANES), 0).astype(jnp.float32)
    for g in range(damping.shape[1] // 8):
        for half in range(HALVES):
            part = damping_ref[half, 8 * g : 8 * g + 8, :]
            for m in range(8):
                powers_ref[8 * half + m, 8 * g : 8 * g + 8, :] = jnp.exp(
                    -spread(part, m) * since
                )


def project(gated, weight_ref, group):
    width = weight_ref.shape[1] // 4
    first = pl.multiple_of((lax.axis_index("ch") ^ group) * width, LANES)
    return jnp.dot(
        gated, weight_ref[:, pl.ds(first, width)], preferred_element_type=jnp.float32
    )


def project_away(gated_ref, weight_ref, group, own_ref, helped_ref):
    rows = own_ref.shape[0] + helped_ref.shape[0]
    skipped = gated_ref.shape[0] - rows
    result = project(gated_ref[skipped:, :], weight_ref, group)
    own_ref[...] = result[: own_ref.shape[0]]
    helped_ref[...] = result[own_ref.shape[0] :]


def gate_kernel(*refs):
    query_ref, local_ref, handed_ref, powers_ref, eight_ref = refs[:5]
    bases, scale_ref, last_ref, arrived, weight_ref = refs[5:7], *refs[7:9], refs[9:12], refs[12]
    gated_ref, own_ref, helped_ref, state_ref = refs[13:]
    far = sum(last_ref[n] * arrived[n][...] for n in range(3))
    for n in range(2):
        state_ref[n] = bases[n][...] + scale_ref[1 + n] * far
    blocks = ((query_ref, local_ref), (handed_ref.at[0], handed_ref.at[1]))

    def body(g, carry):
        block = pl.ds(pl.multiple_of(8 * g, 8), 8)
        columns = pl.ds(pl.multiple_of(LANES * g, LANES), LANES)
        sums = [
            [locals_[i, block, :] for i in range(locals_.shape[0])] for _, locals_ in blocks
        ]
        for half in range(HALVES):
            eight = eight_ref[half, block, :]
            entries = [state_ref[n, half, block, :] for n in range(2)]
            for m in range(8):
                power, factor = powers_ref[8 * half + m, block, :], spread(eight, m)
                for rows, entry in zip(sums, entries):
                    term = spread(entry, m) * power
                    for i in range(len(rows)):
                        rows[i] = rows[i] + term
                        if i + 1 < len(rows):
                            term = term * factor
        gated = [
            queries[i, block, :] * rows[i]
            for (queries, _), rows in zip(blocks, sums)
            for i in range(len(rows))
        ]
        gated_ref[:, columns] = jnp.concatenate(gated, axis=0).astype(jnp.bfloat16)
        return carry

    lax.fori_loop(0, query_ref.shape[1] // 8, body, 0, unroll=2)
    project_away(gated_ref, weight_ref, 3, own_ref, helped_ref)


def rest_kernel(gated_ref, weight_ref, own_ref, helped_ref, sent_ref, home_ref):
    project_away(gated_ref, weight_ref, 2, own_ref, helped_ref)
    rows = home_ref.shape[0]
    sent_ref[...] = project(gated_ref[:rows, :], weight_ref, 1)
    home_ref[...] = project(gated_ref[:rows, :], weight_ref, 0)


def in_turn(one, other):
    ahead = lax.rem(lax.axis_index("ch"), 2) == 0
    return jnp.where(ahead, one, other), jnp.where(ahead, other, one)


def sum_kernel(own_ref, helped_ref, own_core_ref, helped_core_ref, first_ref, second_ref):
    own, helped = own_ref[...] + own_core_ref[...], helped_ref[...] + helped_core_ref[...]
    first_ref[...], second_ref[...] = in_turn(own, helped)


def finish_kernel(home_ref, second_ref, first_ref, core_ref, out_ref):
    own, helped = in_turn(first_ref[...], second_ref[...])
    start = 0
    for away in (helped, own):
        part = pl.ds(start, away.shape[0])
        total = home_ref[part, :] + core_ref[part, :] + away
        out_ref[part, :] = total.astype(jnp.bfloat16)
        start += away.shape[0]


def partner_pairs(size, step):
    return [(i, i ^ step) for i in range(size)]


def along_z(count, turn):
    pairs = []
    for i in range(4 * count):
        z, low = turn((i // 4) % 4, (i // 2) % 2)
        pairs.append((i, i // 16 * 16 + (z % 4) * 4 + low * 2 + i % 2))
    return pairs


def local(value_rows, key_rows, query_rows, pole_weights, damping_speeds, out_weight):
    rows, channels = value_rows.shape
    count = lax.axis_size("seq")
    queries = tiles(query_rows)
    more, below = ((0, MODES, 0), (0, 0, 0)), ((rows, 0, 0), (0, 0, 0))
    keys, values = (lax.pad(one, 0.0, more) for one in (key_rows, value_rows))
    stacked = tiles(keys * values + lax.pad(damping_speeds, 0.0, below))
    gain = tiles(pole_weights * jnp.sqrt(-jnp.expm1(-2.0 * damping_speeds)))
    shape = gain.shape

    def swap(state, axis):
        pairs = [partner_pairs(count, step * 4**axis) for step in STEPS]
        return [lax.ppermute(state, "seq", pair) for pair in pairs]

    def run_total(own, decays, arrived):
        near_by, farthest = arrived[:-1], arrived[-1]
        own = lax.optimization_barrier(own + decays[len(arrived)] * farthest)
        return own + weighed(decays, 1, near_by)

    def weighed(decays, first, terms):
        return sum(decays[first + n] * term for n, term in enumerate(terms))

    state = kernel_call(
        end_state_kernel, f32(*shape), (stacked,), 2_000_000_000, 600_000
    )
    decays_z, own_z = kernel_call(
        lambda *refs: run_own(0, rows, *refs),
        (f32(11, *shape), f32(*shape)),
        (stacked, state),
        1_000_000_000,
        800_000,
    )
    decays_y = kernel_call(
        lambda *refs: run_kernel(1, rows, *refs),
        f32(7, *shape),
        (stacked,),
        1_000_000_000,
        600_000,
    )
    near, handed = kernel_call(
        local_kernel,
        (f32(*queries.shape), f32(2, HANDED, *queries.shape[1:])),
        (stacked, gain, queries),
        3_000_000_000,
        1_500_000,
    )
    last, scale, eight, powers = kernel_call(
        lambda *refs: last_kernel(rows, *refs),
        (f32(3, *shape), f32(3, *shape), f32(*shape), f32(MODES, *shape[1:])),
        (stacked, gain),
        1_000_000_000,
        1_000_000,
    )
    from_z = swap(state, 0)
    total_z = run_total(own_z, decays_z, from_z)
    total_z, *_ = lax.optimization_barrier((total_z, handed, powers))
    handed = lax.ppermute(
        handed, ("seq", "ch"), along_z(count, lambda z, low: (z + 1 - 2 * low, low))
    )
    from_y = swap(total_z, 1)
    total_y = run_total(decays_y[0] * total_z, decays_y, from_y)
    from_x = swap(total_y, 2)
    from_runs = weighed(decays_y, 4, from_y)
    bases = [
        scale[0] * weighed(decays_z, 4, from_z) + scale[1] * from_runs,
        scale[0] * weighed(decays_z, 7, [state] + from_z) + scale[2] * from_runs,
    ]

    width = out_weight.shape[1] // lax.axis_size("ch")
    whole = f32(rows, width)
    away = (f32(rows - 8 * HANDED, width), f32(8 * HANDED, width))
    gated, own_sent, helped_sent = kernel_call(
        gate_kernel,
        (jax.ShapeDtypeStruct((rows + 8 * HANDED, channels), jnp.bfloat16), *away),
        (
            queries,
            near,
            handed,
            powers,
            eight,
            *bases,
            scale,
            last,
            *from_x,
            out_weight,
        ),
        2_000_000_000,
        3_000_000,
        (pltpu.VMEM((2, *shape), jnp.float32),),
    )
    own_kept, helped_kept, home_sent, home_kept = kernel_call(
        rest_kernel, (*away, whole, whole), (gated, out_weight), 1_000_000, 10_000
    )

    def core_swap(one):
        return lax.ppermute(one, "ch", partner_pairs(4, 1))

    first, second = kernel_call(
        sum_kernel,
        away,
        (own_kept, helped_kept, core_swap(own_sent), core_swap(helped_sent)),
        1_000_000,
        10_000,
    )
    first, home_sent = lax.optimization_barrier((first, home_sent))
    pair = along_z(count, lambda z, low: (z, 1 - low))
    other = along_z(count, lambda z, low: (z - 1 + 2 * low, 1 - low))
    mixed = [(pair, other)[i % 2][i] for i in range(len(pair))]
    turned = [(other, pair)[i % 2][i] for i in range(len(pair))]
    second = lax.ppermute(second, ("seq", "ch"), turned)
    first = lax.ppermute(first, ("seq", "ch"), mixed)
    return kernel_call(
        finish_kernel,
        jax.ShapeDtypeStruct((rows, width), jnp.bfloat16),
        (home_kept, second, first, core_swap(home_sent)),
        1_000_000,
        2_000_000,
    )


def solution(mesh):
    in_specs = (
        P("seq", "ch"),
        P("seq", "ch"),
        P("seq", "ch"),
        P(None, "ch"),
        P(None, "ch"),
        P("ch", None),
    )
    return jax.shard_map(
        local, mesh=mesh, in_specs=in_specs, out_specs=P("seq", "ch"), check_vma=False
    )
```

```python
import jax
import jax.numpy as jnp
from jax import lax
from jax.experimental import pallas as pl
from jax.experimental.pallas import tpu as pltpu
from jax.sharding import PartitionSpec as P

MODES = 16
HALVES = MODES // 8
LANES = 128
SCOPE = 12 * 1024 * 1024
STEPS = (1, 3, 2)
HANDED = 8


def tiles(array):
    rows, columns = array.shape
    cut = array.reshape(rows // 8, 8, columns // LANES, LANES)
    return cut.transpose(0, 2, 1, 3).reshape(rows // 8, 8 * (columns // LANES), LANES)


def spread(values, index):
    return jnp.broadcast_to(values[index : index + 1, :], (8, LANES))


def f32(*shape):
    return jax.ShapeDtypeStruct(shape, jnp.float32)


def kernel_call(body, out_shape, inputs, flops, size, scratch=()):
    outs = jax.tree.map(lambda _: pl.BlockSpec(memory_space=pltpu.VMEM), out_shape)
    return pl.pallas_call(
        body,
        out_shape=out_shape,
        in_specs=[pl.BlockSpec(memory_space=pltpu.VMEM)] * len(inputs),
        out_specs=outs,
        scratch_shapes=scratch,
        cost_estimate=pl.CostEstimate(flops=flops, bytes_accessed=size, transcendentals=0),
        compiler_params=pltpu.CompilerParams(vmem_limit_bytes=SCOPE),
    )(*inputs)


def split(stacked_ref):
    outer = stacked_ref.shape[0] - HALVES
    return stacked_ref.at[pl.ds(0, outer)], stacked_ref.at[pl.ds(outer, HALVES)]


def end_state_kernel(stacked_ref, state_ref):
    signal_ref, damping_ref = split(stacked_ref)
    outer, lanes = signal_ref.shape[0], signal_ref.shape[1] // 8
    place = lax.broadcasted_iota(jnp.int32, (8, LANES), 0)
    for g in range(lanes):
        block = pl.ds(8 * g, 8)
        signal = [signal_ref[i, block, :] for i in range(outer)]
        for half in range(HALVES):
            decay = jnp.exp(-damping_ref[half, block, :])
            result = None
            for m in range(8):
                once = spread(decay, m)
                twice = once * once
                four = twice * twice
                eight = four * four
                total = signal[0]
                for i in range(1, outer):
                    total = eight * total + signal[i]
                total = total + once * pltpu.roll(total, 1, 0)
                total = total + twice * pltpu.roll(total, 2, 0)
                total = total + four * pltpu.roll(total, 4, 0)
                if m != 7:
                    total = pltpu.roll(total, m + 1, 0)
                result = total if result is None else jnp.where(place == m, total, result)
            state_ref[half, block, :] = result


def local_kernel(stacked_ref, gain_ref, query_ref, out_ref, handed_ref):
    signal_ref, damping_ref = split(stacked_ref)

    def row(ref, outer, inner):
        return ref[outer, pl.ds(inner, 8, stride=8), :]

    decay = [jnp.exp(-row(damping_ref, m // 8, m % 8)) for m in range(MODES)]
    gain = [row(gain_ref, m // 8, m % 8) for m in range(MODES)]

    def body(outer, state):
        for inner in range(8):
            signal = row(signal_ref, outer, inner)
            state = tuple(decay[m] * state[m] + signal for m in range(MODES))
            terms = [gain[m] * state[m] for m in range(MODES)]
            while len(terms) > 1:
                terms = [terms[n] + terms[n + 1] for n in range(0, len(terms), 2)]
            out_ref[outer, pl.ds(inner, 8, stride=8), :] = terms[0]
        return state

    zero = jnp.zeros((8, LANES), jnp.float32)
    lax.fori_loop(0, signal_ref.shape[0], body, (zero,) * MODES)
    count = handed_ref.shape[1]
    handed_ref[0] = query_ref[0:count]
    handed_ref[1] = out_ref[0:count]


def places():
    at = lax.axis_index("seq")
    return [lax.rem(at, 4), lax.rem(lax.div(at, 4), 4), lax.div(at, 16)]


def helped(z):
    return lax.rem(z + jnp.where(lax.axis_index("ch") < 2, 3, 1), 4)


def entry_decay(damping, target, there):
    ahead = jnp.maximum(target - there - 1, 0).astype(jnp.float32)
    before = (there < target).astype(jnp.float32)
    return jnp.exp(damping * ahead) * before


def run_kernel(axis, rows, stacked_ref, out_ref):
    here = places()[axis]
    damping = split(stacked_ref)[1][...] * (-1.0 * rows * 4**axis)
    for n, step in enumerate((0, *STEPS)):
        there = here ^ step
        out_ref[n] = jnp.exp(damping * (3 - there).astype(jnp.float32))
        if step:
            out_ref[3 + n] = entry_decay(damping, here, there)
        if axis == 0:
            out_ref[7 + n] = entry_decay(damping, helped(here), there)


def run_own(axis, rows, stacked_ref, state_ref, out_ref, own_ref):
    run_kernel(axis, rows, stacked_ref, out_ref)
    own_ref[...] = out_ref[0] * state_ref[...]


def last_kernel(rows, stacked_ref, gain_ref, out_ref, scale_ref, eight_ref, powers_ref):
    z, y, x = places()
    damping_ref = split(stacked_ref)[1]
    damping, gain = damping_ref[...], gain_ref[...]
    scale_ref[0] = gain
    for n, target in enumerate((z, helped(z))):
        scale_ref[1 + n] = gain * jnp.exp(-damping * (target * rows).astype(jnp.float32))
    to_run = jnp.exp(-damping * (4 * y * rows).astype(jnp.float32))
    for n, step in enumerate(STEPS):
        out_ref[n] = to_run * entry_decay(damping * (-16.0 * rows), x, x ^ step)
    eight_ref[...] = jnp.exp(-8.0 * damping)
    since = 1.0 + lax.broadcasted_iota(jnp.int32, (8, LANES), 0).astype(jnp.float32)
    for g in range(damping.shape[1] // 8):
        for half in range(HALVES):
            part = damping_ref[half, 8 * g : 8 * g + 8, :]
            for m in range(8):
                powers_ref[8 * half + m, 8 * g : 8 * g + 8, :] = jnp.exp(
                    -spread(part, m) * since
                )


def project(gated, weight_ref, group):
    width = weight_ref.shape[1] // 4
    first = pl.multiple_of((lax.axis_index("ch") ^ group) * width, LANES)
    return jnp.dot(
        gated, weight_ref[:, pl.ds(first, width)], preferred_element_type=jnp.float32
    )


def project_away(gated_ref, weight_ref, group, own_ref, helped_ref):
    rows = own_ref.shape[0] + helped_ref.shape[0]
    skipped = gated_ref.shape[0] - rows
    result = project(gated_ref[skipped:, :], weight_ref, group)
    own_ref[...] = result[: own_ref.shape[0]]
    helped_ref[...] = result[own_ref.shape[0] :]


def gate_kernel(*refs):
    query_ref, local_ref, handed_ref, powers_ref, eight_ref = refs[:5]
    bases, scale_ref, last_ref, arrived, weight_ref = refs[5:7], *refs[7:9], refs[9:12], refs[12]
    gated_ref, own_ref, helped_ref, state_ref = refs[13:]
    far = sum(last_ref[n] * arrived[n][...] for n in range(3))
    for n in range(2):
        state_ref[n] = bases[n][...] + scale_ref[1 + n] * far
    blocks = ((query_ref, local_ref), (handed_ref.at[0], handed_ref.at[1]))

    def body(g, carry):
        block = pl.ds(pl.multiple_of(8 * g, 8), 8)
        columns = pl.ds(pl.multiple_of(LANES * g, LANES), LANES)
        sums = [
            [locals_[i, block, :] for i in range(locals_.shape[0])] for _, locals_ in blocks
        ]
        for half in range(HALVES):
            eight = eight_ref[half, block, :]
            entries = [state_ref[n, half, block, :] for n in range(2)]
            for m in range(8):
                power, factor = powers_ref[8 * half + m, block, :], spread(eight, m)
                for rows, entry in zip(sums, entries):
                    term = spread(entry, m) * power
                    for i in range(len(rows)):
                        rows[i] = rows[i] + term
                        if i + 1 < len(rows):
                            term = term * factor
        gated = [
            queries[i, block, :] * rows[i]
            for (queries, _), rows in zip(blocks, sums)
            for i in range(len(rows))
        ]
        gated_ref[:, columns] = jnp.concatenate(gated, axis=0).astype(jnp.bfloat16)
        return carry

    lax.fori_loop(0, query_ref.shape[1] // 8, body, 0, unroll=2)
    project_away(gated_ref, weight_ref, 3, own_ref, helped_ref)


def rest_kernel(gated_ref, weight_ref, own_ref, helped_ref, sent_ref, home_ref):
    project_away(gated_ref, weight_ref, 2, own_ref, helped_ref)
    rows = home_ref.shape[0]
    sent_ref[...] = project(gated_ref[:rows, :], weight_ref, 1)
    home_ref[...] = project(gated_ref[:rows, :], weight_ref, 0)


def in_turn(one, other):
    ahead = lax.rem(lax.axis_index("ch"), 2) == 1
    return jnp.where(ahead, one, other), jnp.where(ahead, other, one)


def sum_kernel(own_ref, helped_ref, own_core_ref, helped_core_ref, first_ref, second_ref):
    own, helped = own_ref[...] + own_core_ref[...], helped_ref[...] + helped_core_ref[...]
    first_ref[...], second_ref[...] = in_turn(own, helped)


def finish_kernel(home_ref, second_ref, first_ref, core_ref, out_ref):
    own, helped = in_turn(first_ref[...], second_ref[...])
    start = 0
    for away in (helped, own):
        part = pl.ds(start, away.shape[0])
        total = home_ref[part, :] + core_ref[part, :] + away
        out_ref[part, :] = total.astype(jnp.bfloat16)
        start += away.shape[0]


def partner_pairs(size, step):
    return [(i, i ^ step) for i in range(size)]


def along_z(count, turn):
    pairs = []
    for i in range(4 * count):
        z, low = turn((i // 4) % 4, (i // 2) % 2)
        pairs.append((i, i // 16 * 16 + (z % 4) * 4 + low * 2 + i % 2))
    return pairs


def local(value_rows, key_rows, query_rows, pole_weights, damping_speeds, out_weight):
    rows, channels = value_rows.shape
    count = lax.axis_size("seq")
    queries = tiles(query_rows)
    more, below = ((0, MODES, 0), (0, 0, 0)), ((rows, 0, 0), (0, 0, 0))
    keys, values = (lax.pad(one, 0.0, more) for one in (key_rows, value_rows))
    stacked = tiles(keys * values + lax.pad(damping_speeds, 0.0, below))
    gain = tiles(pole_weights * jnp.sqrt(-jnp.expm1(-2.0 * damping_speeds)))
    shape = gain.shape

    def swap(state, axis):
        pairs = [partner_pairs(count, step * 4**axis) for step in STEPS]
        return [lax.ppermute(state, "seq", pair) for pair in pairs]

    def run_total(own, decays, arrived):
        near_by, farthest = arrived[:-1], arrived[-1]
        own = lax.optimization_barrier(own + decays[len(arrived)] * farthest)
        return own + weighed(decays, 1, near_by)

    def weighed(decays, first, terms):
        return sum(decays[first + n] * term for n, term in enumerate(terms))

    state = kernel_call(
        end_state_kernel, f32(*shape), (stacked,), 2_000_000_000, 600_000
    )
    decays_z, own_z = kernel_call(
        lambda *refs: run_own(0, rows, *refs),
        (f32(11, *shape), f32(*shape)),
        (stacked, state),
        1_000_000_000,
        800_000,
    )
    decays_y = kernel_call(
        lambda *refs: run_kernel(1, rows, *refs),
        f32(7, *shape),
        (stacked,),
        1_000_000_000,
        600_000,
    )
    near, handed = kernel_call(
        local_kernel,
        (f32(*queries.shape), f32(2, HANDED, *queries.shape[1:])),
        (stacked, gain, queries),
        3_000_000_000,
        1_500_000,
    )
    last, scale, eight, powers = kernel_call(
        lambda *refs: last_kernel(rows, *refs),
        (f32(3, *shape), f32(3, *shape), f32(*shape), f32(MODES, *shape[1:])),
        (stacked, gain),
        1_000_000_000,
        1_000_000,
    )
    from_z = swap(state, 0)
    total_z = run_total(own_z, decays_z, from_z)
    total_z, *_ = lax.optimization_barrier((total_z, handed, powers))
    handed = lax.ppermute(
        handed, ("seq", "ch"), along_z(count, lambda z, low: (z + 1 - 2 * low, low))
    )
    from_y = swap(total_z, 1)
    total_y = run_total(decays_y[0] * total_z, decays_y, from_y)
    from_x = swap(total_y, 2)
    from_runs = weighed(decays_y, 4, from_y)
    bases = [
        scale[0] * weighed(decays_z, 4, from_z) + scale[1] * from_runs,
        scale[0] * weighed(decays_z, 7, [state] + from_z) + scale[2] * from_runs,
    ]

    width = out_weight.shape[1] // lax.axis_size("ch")
    whole = f32(rows, width)
    away = (f32(rows - 8 * HANDED, width), f32(8 * HANDED, width))
    gated, own_sent, helped_sent = kernel_call(
        gate_kernel,
        (jax.ShapeDtypeStruct((rows + 8 * HANDED, channels), jnp.bfloat16), *away),
        (
            queries,
            near,
            handed,
            powers,
            eight,
            *bases,
            scale,
            last,
            *from_x,
            out_weight,
        ),
        2_000_000_000,
        3_000_000,
        (pltpu.VMEM((2, *shape), jnp.float32),),
    )
    own_kept, helped_kept, home_sent, home_kept = kernel_call(
        rest_kernel, (*away, whole, whole), (gated, out_weight), 1_000_000, 10_000
    )

    def core_swap(one):
        return lax.ppermute(one, "ch", partner_pairs(4, 1))

    first, second = kernel_call(
        sum_kernel,
        away,
        (own_kept, helped_kept, core_swap(own_sent), core_swap(helped_sent)),
        1_000_000,
        10_000,
    )
    pair = along_z(count, lambda z, low: (z, 1 - low))
    other = along_z(count, lambda z, low: (z - 1 + 2 * low, 1 - low))
    mixed = [(other, pair)[i % 2][i] for i in range(len(pair))]
    turned = [(pair, other)[i % 2][i] for i in range(len(pair))]
    second = lax.ppermute(second, ("seq", "ch"), turned)
    first = lax.ppermute(first, ("seq", "ch"), mixed)
    return kernel_call(
        finish_kernel,
        jax.ShapeDtypeStruct((rows, width), jnp.bfloat16),
        (home_kept, second, first, core_swap(home_sent)),
        1_000_000,
        2_000_000,
    )


def solution(mesh):
    in_specs = (
        P("seq", "ch"),
        P("seq", "ch"),
        P("seq", "ch"),
        P(None, "ch"),
        P(None, "ch"),
        P("ch", None),
    )
    return jax.shard_map(
        local, mesh=mesh, in_specs=in_specs, out_specs=P("seq", "ch"), check_vma=False
    )
```
